512 devices in a mesh: dp: 64 (over x, z_lo, core), tensor: 8 (over z_hi, y).
Axes of the slice: x: 4, y: 4, z: 16 (z_hi: 2, z_lo: 8; z = z_hi * 8 + z_lo), core: 2. Of those that a mesh axis runs over, the one named last changes fastest.
Arguments:
- image_pooled: bfloat16 [8192, 1408], P('dp'), may hold values from -6 to 6
- text_pooled: bfloat16 [8192, 1408], P('dp'), may hold values from -6 to 6
- image_proj: bfloat16 [1152, 1408], P('tensor'), may hold values from -0.15625 to 0.15625
- text_proj: bfloat16 [1152, 1408], P('tensor'), may hold values from -0.15625 to 0.15625
- logit_scale: float32 [], replicated, may hold values from 4 to 12
- logit_bias: float32 [], replicated, may hold values from -5 to -1
Outputs:
- loss: float32 [], replicated
- grad_scale: float32 [], replicated
- grad_bias: float32 [], replicated
- grad_image_proj: float32 [1152, 1408], P('tensor')
- grad_text_proj: float32 [1152, 1408], P('tensor')
The draws below stay inside these ranges and needn't reach their ends.
All inputs are finite; a program needn't handle non-finite values.
Results may differ from the reference program's by a relative error of at most 0.004.
Values may be sent and summed in bfloat16 or wider, within the bound.
No kernel may reach another device: no remote copies, remote signals or barrier semaphores. Data moves between devices by JAX's collectives and lax.ppermute only.
A program may use at most 64 MiB of HBM per device.

```python
import jax
import jax.numpy as jnp
from jax import lax

WIDTH = 1408
EMB = 1152
B_DEV = 128
BATCH = 8192


def level_of(rng, extent, shards, low, high):
    def one(dim, blocks):
        heights = jax.random.uniform(jax.random.fold_in(jax.random.fold_in(rng, 6), dim), (blocks,), jnp.float32, low / len(shards), high / len(shards))
        return jnp.repeat(jnp.exp(heights), extent[dim] // blocks).reshape((-1,) + (1,) * (len(extent) - dim - 1))

    loudness = one(*shards[0])
    for cut in shards[1:]:
        loudness = loudness * one(*cut)
    return loudness


def noise(stream_key, extent, scale, most, cuts=(), kind=jnp.bfloat16):
    drawn = scale * jax.random.normal(stream_key, extent, jnp.float32)
    if cuts:
        drawn = drawn * level_of(stream_key, extent, cuts, -0.22, 0.18)
    return jnp.clip(drawn, -most, most).astype(kind)


def setup_inputs(seed: int = 0) -> dict:
    seeds = jax.random.split(jax.random.key(seed), 7)
    return {
        "image_pooled": noise(seeds[0], (BATCH, WIDTH), 1.0, 6.0, ((0, 64),)),
        "text_pooled": noise(seeds[1], (BATCH, WIDTH), 1.0, 6.0, ((0, 64),)),
        "image_proj": noise(seeds[2], (EMB, WIDTH), WIDTH ** -0.5, 0.15625, ((0, 8),)),
        "text_proj": noise(seeds[3], (EMB, WIDTH), WIDTH ** -0.5, 0.15625, ((0, 8),)),
        "logit_scale": jnp.clip(jax.random.uniform(seeds[4], (), jnp.float32, 4.0, 12.0), 4.0, 12.0),
        "logit_bias": jnp.clip(jax.random.uniform(seeds[5], (), jnp.float32, -5.0, -1.0), -5.0, -1.0),
    }


eps = 1e-06

def embed(pooled, proj):
    raw = lax.dot_general(pooled, proj, (((1,), (1,)), ((), ())), preferred_element_type=jnp.float32)
    norm = jnp.sqrt(lax.optimization_barrier(jnp.sum(raw * raw, axis=1, keepdims=True)) + eps)
    unit = raw / norm
    return (unit, norm, unit.astype(jnp.bfloat16))

def backprop(pooled, unit, norm, demb):
    inner = lax.optimization_barrier(jnp.sum(unit * demb, axis=1, keepdims=True))
    draw = (demb - unit * inner) / norm
    dlow = draw.astype(jnp.bfloat16)
    return lax.dot_general(dlow, pooled, (((0,), (0,)), ((), ())), preferred_element_type=jnp.float32)

def reference(image_pooled, text_pooled, image_proj, text_proj, logit_scale, logit_bias):
    total = image_pooled.shape[0]
    image_unit, image_norm, image_emb = embed(image_pooled, image_proj)
    text_unit, text_norm, text_emb = embed(text_pooled, text_proj)
    columns = jnp.arange(total, dtype=jnp.int32)
    rowpos = jnp.arange(B_DEV, dtype=jnp.int32)

    def block_step(carry, index):
        text_demb, loss, grad_scale, grad_bias = carry
        start = index * B_DEV
        block = lax.dynamic_slice_in_dim(image_emb, start, B_DEV, 0)
        dots = lax.dot_general(block, text_emb, (((1,), (1,)), ((), ())), preferred_element_type=jnp.float32)
        logits = logit_scale * dots + logit_bias
        label = jnp.where(rowpos[:, None] + start == columns[None, :], jnp.float32(1.0), jnp.float32(-1.0))
        loss = loss - jnp.sum(jax.nn.log_sigmoid(label * logits)) / total
        pair_grad = -label * jax.nn.sigmoid(-label * logits) / total
        grad_scale = grad_scale + jnp.sum(pair_grad * dots)
        grad_bias = grad_bias + jnp.sum(pair_grad)
        coef = (logit_scale * pair_grad).astype(jnp.bfloat16)
        image_part = jnp.dot(coef, text_emb, preferred_element_type=jnp.float32)
        text_demb = text_demb + lax.dot_general(coef, block, (((0,), (0,)), ((), ())), preferred_element_type=jnp.float32)
        return ((text_demb, loss, grad_scale, grad_bias), image_part)
    start_carry = (jnp.zeros(text_emb.shape, jnp.float32), jnp.float32(0.0), jnp.float32(0.0), jnp.float32(0.0))
    carry, parts = lax.scan(block_step, start_carry, jnp.arange(total // B_DEV, dtype=jnp.int32))
    text_demb, loss, grad_scale, grad_bias = carry
    image_demb = parts.reshape(total, image_emb.shape[1])
    grad_image_proj = backprop(image_pooled, image_unit, image_norm, image_demb)
    grad_text_proj = backprop(text_pooled, text_unit, text_norm, text_demb)
    return (loss, grad_scale, grad_bias, grad_image_proj, grad_text_proj)
```

```python
import jax
import jax.numpy as jnp
from jax import lax
from jax.sharding import Mesh, PartitionSpec as P

eps = 1e-06
X, ZL, CORE, ZH, Y = 4, 8, 2, 2, 4
AXES = ("x", "zl", "core", "zh", "y")


def swap(block, axis):
    return lax.ppermute(block, axis, [(0, 1), (1, 0)])


def by_core(block):
    other = swap(block, "core")
    first = lax.axis_index("core") == 0
    return jnp.stack([jnp.where(first, block, other), jnp.where(first, other, block)])


def spread(block, axes, count):
    copies = jnp.broadcast_to(block[None], (count,) + block.shape)
    return lax.all_to_all(copies, axes, 0, 0, tiled=True)


def in_parts(value):
    high = value.astype(jnp.bfloat16)
    rest = value - high.astype(jnp.float32)
    mid = rest.astype(jnp.bfloat16)
    low = (rest - mid.astype(jnp.float32)).astype(jnp.bfloat16)
    return jnp.stack([high, mid, low])


def shards(image_pooled, text_pooled, image_proj, text_proj, logit_scale, logit_bias):
    bf16, f32 = jnp.bfloat16, jnp.float32
    x, zl, core, zh, y = [lax.axis_index(a) for a in AXES]
    rows, width = image_pooled.shape
    feats = image_proj.shape[0]
    total = rows * X * ZL * CORE
    half, quarter, eighth = rows // ZH, rows // Y, rows // (Y * ZH)
    fhalf = feats // CORE
    emb = feats * ZH * Y

    image_rows = lax.dynamic_slice_in_dim(image_pooled, zh * half, half, 0)
    image_rows = lax.all_gather(image_rows, ("x", "core"), axis=0, tiled=True)
    text_rows = lax.dynamic_slice_in_dim(text_pooled, y * quarter + zh * eighth, eighth, 0)
    text_rows = lax.all_gather(text_rows, ("zh", "zl"), axis=0, tiled=True)
    text_rows = by_core(text_rows).reshape(CORE, ZH, ZL, eighth, width)
    text_rows = text_rows.transpose(2, 0, 1, 3, 4).reshape(ZL * CORE * quarter, width)

    def raw_of(proj, pooled):
        return lax.dot_general(
            proj, pooled, (((1,), (1,)), ((), ())), preferred_element_type=f32
        ).astype(bf16)

    image_raw = raw_of(image_proj, image_pooled)
    text_raw = raw_of(text_proj, text_pooled)
    image_raw = image_raw.reshape(CORE, fhalf, ZH, half).transpose(2, 1, 0, 3).reshape(ZH, fhalf, rows)
    mine = lax.dynamic_index_in_dim(image_raw, zh, 0, keepdims=False)
    away = lax.dynamic_index_in_dim(image_raw, 1 - zh, 0, keepdims=False)
    back = swap(away, "zh")
    text_raw = text_raw.reshape(Y, feats // Y, Y, quarter).transpose(2, 1, 0, 3)
    text_raw = lax.all_to_all(text_raw.reshape(Y * (feats // Y), rows), "y", 0, 0, tiled=True)
    text_raw = lax.all_gather(text_raw, ("zh", "zl"), axis=0, tiled=True)
    text_raw = by_core(text_raw).reshape(CORE, ZH, ZL, Y, feats // Y, Y, quarter)
    text_raw = text_raw.transpose(1, 3, 5, 4, 2, 0, 6).reshape(emb, ZL * CORE * quarter)

    low = zh == 0
    image_raw = jnp.concatenate([jnp.where(low, mine, back), jnp.where(low, back, mine)], 0)
    image_raw = spread(image_raw, ("x", "y"), X * Y)
    image_raw = by_core(image_raw).reshape(CORE, X, Y, ZH, fhalf, CORE, half)
    image_raw = image_raw.transpose(3, 2, 5, 4, 1, 0, 6).reshape(emb, X * CORE * half)

    n_images, n_texts = image_raw.shape[1], text_raw.shape[1]
    wide = image_raw.astype(f32)
    image_inv = 1.0 / jnp.sqrt(jnp.sum(wide * wide, axis=0) + eps)
    wide = text_raw.astype(f32)
    text_inv = 1.0 / jnp.sqrt(jnp.sum(wide * wide, axis=0) + eps)

    i = jnp.arange(n_images, dtype=jnp.int32)
    j = jnp.arange(n_texts, dtype=jnp.int32)
    ix, icore, irow = i // (CORE * half), i // half % CORE, i % half
    jz, jcore, jrow = j // (CORE * quarter), j // quarter % CORE, j % quarter
    image_id = ((ix * ZL + zl) * CORE + icore) * rows + zh * half + irow
    text_id = ((x * ZL + jz) * CORE + jcore) * rows + y * quarter + jrow

    dots = lax.dot_general(
        image_raw, text_raw, (((0,), (0,)), ((), ())), preferred_element_type=f32
    )
    dots = dots * (image_inv[:, None] * text_inv[None, :])
    logits = logit_scale * dots + logit_bias
    label = jnp.where(image_id[:, None] == text_id[None, :], f32(1.0), f32(-1.0))
    loss = -jnp.sum(jax.nn.log_sigmoid(label * logits)) / total
    pair_grad = -label * jax.nn.sigmoid(-label * logits) / total
    grad_scale = jnp.sum(pair_grad * dots)
    grad_bias = jnp.sum(pair_grad)
    coef = logit_scale * pair_grad
    inner = coef * dots
    image_inner = jnp.sum(inner, axis=1)
    text_inner = jnp.sum(inner, axis=0)

    def own(raw):
        raw = raw.reshape(ZH * Y, feats, raw.shape[1])
        return lax.dynamic_slice_in_dim(raw, core * fhalf, fhalf, 1).reshape(emb // CORE, -1)

    image_own, text_own = own(image_raw), own(text_raw)
    image_draw = lax.dot_general(
        text_own, (coef * text_inv[None, :]).astype(bf16), (((1,), (1,)), ((), ())),
        preferred_element_type=f32,
    )
    image_draw = (image_draw - image_own.astype(f32) * (image_inner * image_inv)) * image_inv
    text_draw = jnp.dot(
        image_own, (coef * image_inv[:, None]).astype(bf16), preferred_element_type=f32
    )
    text_draw = (text_draw - text_own.astype(f32) * (text_inner * text_inv)) * text_inv
    image_w = jnp.dot(image_draw.astype(bf16), image_rows, preferred_element_type=f32)
    text_w = jnp.dot(text_draw.astype(bf16), text_rows, preferred_element_type=f32)

    sums = jnp.concatenate([in_parts(v) for v in (loss, grad_scale, grad_bias)])
    tail = jnp.zeros((8, width), bf16).at[0, :9].set(sums)
    tail = jnp.broadcast_to(tail, (X, Y, 8, width))
    parts = jnp.concatenate([image_w.astype(bf16), text_w.astype(bf16)])
    parts = jnp.concatenate([parts.reshape(X, Y, fhalf, width), tail], axis=2)
    parts = lax.all_to_all(
        parts.reshape(X * Y, fhalf + 8, width), ("x", "y"), 0, 0, tiled=True
    )
    parts = jnp.sum(parts.astype(f32), axis=0)
    tiles = parts[:fhalf].reshape(fhalf // 8, 8, width // 128, 128).transpose(0, 2, 1, 3)
    count = (fhalf // 8) * (width // 128)
    share = -(-count // ZL)
    tiles = jnp.pad(tiles.reshape(count, 8, 128), ((0, share * ZL - count), (0, 0), (0, 0)))
    tail = jnp.broadcast_to(parts[None, None, fhalf:, :128], (ZL, 1, 8, 128))
    tiles = jnp.concatenate([tiles.reshape(ZL, share, 8, 128), tail], axis=1)
    tiles = lax.all_to_all(tiles, "zl", 0, 0, tiled=True)
    tiles = jnp.sum(tiles, axis=0)
    tiles = tiles + swap(tiles, "zh")
    sums = tiles[share, 0, :9].reshape(3, 3).sum(axis=1)
    tiles = spread(tiles[:share], "zl", ZL)
    pieces = []
    for steps in (((0, 1), (2, 3)), ((0, 3), (2, 1)), ((0, 2), (2, 0))):
        route = [((s + h) * ZH + h, ((t + h) % X) * ZH + h) for s, t in steps for h in range(ZH)]
        pieces.append(lax.ppermute(tiles, ("x", "zh"), route))
    near, far, across = pieces
    place = (x - zh) % X
    image_g = jnp.where(place == 0, tiles, jnp.where(place == 1, near, jnp.where(place == 2, across, far)))
    text_g = jnp.where(place == 2, tiles, jnp.where(place == 3, near, jnp.where(place == 0, across, far)))
    both = jnp.stack([image_g, text_g]).reshape(2, ZL * share, 8, 128)[:, :count]
    both = by_core(both).reshape(CORE, 2, fhalf // 8, width // 128, 8, 128)
    both = both.transpose(1, 0, 2, 4, 3, 5).reshape(2, feats, width)
    return (sums[0], sums[1], sums[2], both[0], both[1])


def solution(mesh):
    fine = Mesh(mesh.devices.reshape(X, ZL, CORE, ZH, Y), AXES)
    dp, tensor = ("x", "zl", "core"), ("zh", "y")
    placed = (P(dp, None), P(dp, None), P(tensor, None), P(tensor, None), P(), P())
    return jax.shard_map(
        shards,
        mesh=fine,
        in_specs=placed,
        out_specs=(P(), P(), P(), P(tensor, None), P(tensor, None)),
        check_vma=False,
    )
```

```python
import jax
import jax.numpy as jnp
from jax import lax
from jax.experimental import pallas as pl
from jax.experimental.pallas import tpu as pltpu
from jax.sharding import Mesh, PartitionSpec as P

eps = 1e-06
X, ZL, CORE, ZH, Y = 4, 8, 2, 2, 4
AXES = ("x", "zl", "core", "zh", "y")
TAIL = 16


def swap(block, axis):
    return lax.ppermute(block, axis, [(0, 1), (1, 0)])


def spread(block, axes, count):
    copies = jnp.broadcast_to(block[None], (count,) + block.shape)
    return lax.all_to_all(copies, axes, 0, 0, tiled=True)


def in_parts(value):
    high = value.astype(jnp.bfloat16).astype(jnp.float32)
    rest = value - high
    mid = rest.astype(jnp.bfloat16).astype(jnp.float32)
    return high, mid, rest - mid


def pairs_kernel(
    place, factors, plane, ring_mine, ring_other, out, plane_raw, ring_raw
):
    bf16, f32 = jnp.bfloat16, jnp.float32
    core, x, y, zl, zh = [place[k] for k in range(5)]
    scale, bias = factors[0], factors[1]
    feats, rows = ring_mine.shape[1:]
    emb, block = ring_raw.shape
    own = emb // ZH
    total = rows * X * ZL * CORE

    for s in range(X * Y):
        for g in range(CORE):
            lanes = pl.ds((s // Y * CORE + g) * rows, rows)
            for h in range(ZH):
                piece = plane[s, pl.ds((g * ZH + h) * feats, feats), :]
                plane_raw[pl.ds((h * Y + s % Y) * feats, feats), lanes] = piece
    for ref, owner in ((ring_mine, core), (ring_other, 1 - core)):
        for s in range(ZH * ZL):
            at = (s // ZL * Y + s % Y) * feats
            lanes = pl.multiple_of((s % ZL // Y * CORE + owner) * rows, rows)
            ring_raw[pl.ds(at, feats), pl.ds(lanes, rows)] = ref[s]

    wide = ring_raw[...].astype(f32)
    ring_inv = 1.0 / jnp.sqrt(jnp.sum(wide * wide, axis=0, keepdims=True) + eps)
    own_at = pl.multiple_of(zh * own, 16)
    ring_own = ring_raw[pl.ds(own_at, own), :]

    lane = lax.broadcasted_iota(jnp.int32, (rows, block), 1)
    row = lax.broadcasted_iota(jnp.int32, (rows, block), 0)
    ring_id = ((x * ZL + 2 * y) * CORE + lane // rows) * rows + lane % rows
    loss = grad_scale = grad_bias = jnp.zeros((1, block), f32)
    for a in range(X * CORE):
        images = plane_raw[:, pl.ds(a * rows, rows)].T
        wide = images.astype(f32)
        inv = 1.0 / jnp.sqrt(jnp.sum(wide * wide, axis=1, keepdims=True) + eps)
        dots = jnp.dot(images, ring_raw[...], preferred_element_type=f32) * inv * ring_inv
        logits = scale * dots + bias
        plane_id = ((a // CORE * ZL + zl) * CORE + a % CORE) * rows + row
        label = jnp.where(plane_id == ring_id, f32(1.0), f32(-1.0))
        margin = label * logits
        small = jnp.exp(-jnp.abs(margin))
        sigmoid = jnp.where(margin >= 0, small, 1.0) / (1.0 + small)
        pair_grad = -label * sigmoid * f32(1.0 / total)
        inner = pair_grad * dots
        loss += jnp.sum(jnp.log1p(small) - jnp.minimum(margin, 0.0), axis=0, keepdims=True)
        grad_scale += jnp.sum(inner, axis=0, keepdims=True)
        grad_bias += jnp.sum(pair_grad, axis=0, keepdims=True)
        shift = scale * jnp.sum(inner, axis=1, keepdims=True) * inv
        shift = jnp.broadcast_to(shift, (rows, rows)).T[:1]
        inv = jnp.broadcast_to(inv, (rows, rows)).T[:1]
        coef = (scale * pair_grad * ring_inv).astype(bf16)
        draw = lax.dot_general(
            ring_own, coef, (((1,), (1,)), ((), ())), preferred_element_type=f32
        )
        raw = plane_raw[pl.ds(own_at, own), pl.ds(a * rows, rows)].astype(f32)
        draw = ((draw - raw * shift) * inv).astype(bf16)
        for b in range(Y):
            part = draw[b * feats : (b + 1) * feats]
            out[a // CORE * Y + b, pl.ds(0, feats), pl.ds(a % CORE * rows, rows)] = part

    lane = lax.broadcasted_iota(jnp.int32, (TAIL, CORE * rows), 1)
    tail = jnp.zeros((TAIL, CORE * rows), f32)
    for k, value in enumerate((loss * f32(1.0 / total), grad_scale, grad_bias)):
        for n, part in enumerate(in_parts(jnp.sum(value, axis=1, keepdims=True))):
            tail = jnp.where(lane == 3 * k + n, part, tail)
    for s in range(X * Y):
        out[s, pl.ds(feats, TAIL), :] = tail.astype(bf16)


def row_gradients(place, factors, plane, ring, ring_other):
    feats, rows = ring.shape[1:]
    smem, vmem = pl.BlockSpec(memory_space=pltpu.SMEM), pl.BlockSpec(memory_space=pltpu.VMEM)
    emb, block = feats * ZH * Y, rows * X
    return pl.pallas_call(
        pairs_kernel,
        out_shape=jax.ShapeDtypeStruct((X * Y, feats + TAIL, CORE * rows), jnp.bfloat16),
        in_specs=[smem] * 2 + [vmem] * 3,
        out_specs=vmem,
        scratch_shapes=[
            pltpu.VMEM((emb, CORE * block), jnp.bfloat16),
            pltpu.VMEM((emb, block), jnp.bfloat16),
        ],
        compiler_params=pltpu.CompilerParams(vmem_limit_bytes=48 * 1024 * 1024),
    )(place, factors, plane, ring, ring_other)


def shards(image_pooled, text_pooled, image_proj, text_proj, logit_scale, logit_bias):
    bf16, f32 = jnp.bfloat16, jnp.float32
    x, zl, core, zh, y = [lax.axis_index(a) for a in AXES]
    width = image_pooled.shape[1]
    feats = image_proj.shape[0]
    place = jnp.stack([core, x, y, zl, zh]).astype(jnp.int32)
    factors = jnp.stack([logit_scale, logit_bias])
    first = core == 0

    def raw_of(proj, pooled):
        return lax.dot_general(
            proj, pooled, (((1,), (1,)), ((), ())), preferred_element_type=f32
        ).astype(bf16)

    to_ring = [(p * Y + q, (p % 2 * Y + q) * Y + p // 2) for p in range(ZL) for q in range(Y)]
    pooled = jnp.where(first, image_pooled, text_pooled)
    beside = swap(jnp.where(first, text_pooled, image_pooled), "core")
    pooled = jnp.concatenate([jnp.where(first, pooled, beside), jnp.where(first, beside, pooled)])
    image_raw, text_raw = raw_of(image_proj, image_pooled), raw_of(text_proj, text_pooled)
    mine, theirs = jnp.where(first, image_raw, text_raw), jnp.where(first, text_raw, image_raw)
    raw = jnp.concatenate([mine, theirs])
    ring = lax.ppermute(raw, ("zl", "y"), to_ring)
    far = swap(raw, "zh")
    low = zh == 0

    def both_zh(here, there):
        return jnp.concatenate([jnp.where(low, here, there), jnp.where(low, there, here)])

    beside = swap(both_zh(theirs, far[feats:]), "core")
    ring_first, ring_second = ring[feats:], swap(ring[:feats], "core")
    plane = both_zh(mine, far[:feats])
    plane = jnp.concatenate([jnp.where(first, plane, beside), jnp.where(first, beside, plane)])
    plane, ring_first, ring_second = lax.optimization_barrier((plane, ring_first, ring_second))
    plane = spread(plane, ("x", "y"), X * Y)
    ring_first = lax.all_gather(ring_first, ("zh", "zl"), axis=0, tiled=False)
    ring_second = lax.all_gather(ring_second, ("zh", "zl"), axis=0, tiled=False)
    plane, ring_first, ring_second = lax.optimization_barrier((plane, ring_first, ring_second))
    parts = row_gradients(place, factors, plane, ring_first, ring_second)
    parts = lax.all_to_all(parts, ("x", "y"), 0, 0, tiled=True)
    parts = jnp.sum(parts.astype(f32), axis=0)
    draw, tail = parts[:feats].astype(bf16), parts[feats : feats + 8, :128]

    weight = jnp.dot(draw, pooled, preferred_element_type=f32)

    count = (feats // 8) * (width // 128)
    share = -(-count // (X * ZL))
    tiles = weight.reshape(feats // 8, 8, width // 128, 128).transpose(0, 2, 1, 3)
    tiles = jnp.pad(tiles.reshape(count, 8, 128), ((0, X * ZL * share - count), (0, 0), (0, 0)))
    tiles = lax.all_to_all(tiles.reshape(X, ZL * share, 8, 128), "x", 0, 0, tiled=True)
    tiles = jnp.sum(tiles, axis=0).reshape(ZL, share, 8, 128)
    tiles = jnp.concatenate([tiles, jnp.broadcast_to(tail, (ZL, 1, 8, 128))], axis=1)
    tiles = jnp.sum(lax.all_to_all(tiles, "zl", 0, 0, tiled=True), axis=0)
    tail = tiles[share]
    tail = jnp.where(first, tail, swap(tail, "core"))
    sums = tail[0, :9].reshape(3, 3).sum(axis=1)
    tiles = spread(tiles[:share].astype(bf16), "zl", ZL)
    tiles = lax.all_gather(tiles, "x", axis=0, tiled=False)
    other = swap(tiles, "core")

    def whole(tiles):
        tiles = tiles.reshape(X * ZL * share, 8, 128)[:count]
        tiles = tiles.reshape(feats // 8, width // 128, 8, 128).transpose(0, 2, 1, 3)
        return tiles.reshape(feats, width).astype(f32)

    image_grad = whole(jnp.where(first, tiles, other))
    text_grad = whole(jnp.where(first, other, tiles))
    return (sums[0], sums[1], sums[2], image_grad, text_grad)


def solution(mesh):
    fine = Mesh(mesh.devices.reshape(X, ZL, CORE, ZH, Y), AXES)
    dp, tensor = ("x", "zl", "core"), ("zh", "y")
    placed = (P(dp, None), P(dp, None), P(tensor, None), P(tensor, None), P(), P())
    return jax.shard_map(
        shards,
        mesh=fine,
        in_specs=placed,
        out_specs=(P(), P(), P(), P(tensor, None), P(tensor, None)),
        check_vma=False,
    )
```

```python
import jax
import jax.numpy as jnp
from jax import lax
from jax.experimental import pallas as pl
from jax.experimental.pallas import tpu as pltpu
from jax.sharding import Mesh, PartitionSpec as P

eps = 1e-06
X, ZL, CORE, ZH, Y = 4, 8, 2, 2, 4
AXES = ("x", "zl", "core", "zh", "y")
TAIL = 16


def swap(block, axis):
    return lax.ppermute(block, axis, [(0, 1), (1, 0)])


def spread(block, axes, count):
    copies = jnp.broadcast_to(block[None], (count,) + block.shape)
    return lax.all_to_all(copies, axes, 0, 0, tiled=True)


def in_parts(value):
    high = value.astype(jnp.bfloat16).astype(jnp.float32)
    rest = value - high
    mid = rest.astype(jnp.bfloat16).astype(jnp.float32)
    return high, mid, rest - mid


def pairs_kernel(
    place, factors, plane, ring_mine, ring_other, out, plane_raw, ring_raw
):
    bf16, f32 = jnp.bfloat16, jnp.float32
    core, x, y, zl, zh = [place[k] for k in range(5)]
    scale, bias = factors[0], factors[1]
    feats, rows = ring_mine.shape[1:]
    emb, block = ring_raw.shape
    own = emb // ZH
    total = rows * X * ZL * CORE

    for s in range(X * Y):
        for g in range(CORE):
            lanes = pl.ds((s // Y * CORE + g) * rows, rows)
            for h in range(ZH):
                piece = plane[s, pl.ds((g * ZH + h) * feats, feats), :]
                plane_raw[pl.ds((h * Y + s % Y) * feats, feats), lanes] = piece
    for ref, owner in ((ring_mine, core), (ring_other, 1 - core)):
        for s in range(ZH * ZL):
            at = (s // ZL * Y + s % Y) * feats
            lanes = pl.multiple_of((s % ZL // Y * CORE + owner) * rows, rows)
            ring_raw[pl.ds(at, feats), pl.ds(lanes, rows)] = ref[s]

    wide = ring_raw[...].astype(f32)
    ring_inv = 1.0 / jnp.sqrt(jnp.sum(wide * wide, axis=0, keepdims=True) + eps)
    own_at = pl.multiple_of(zh * own, 16)
    ring_own = ring_raw[pl.ds(own_at, own), :]

    lane = lax.broadcasted_iota(jnp.int32, (rows, block), 1)
    row = lax.broadcasted_iota(jnp.int32, (rows, block), 0)
    ring_id = ((x * ZL + 2 * y) * CORE + lane // rows) * rows + lane % rows
    loss = grad_scale = grad_bias = jnp.zeros((1, block), f32)
    for a in range(X * CORE):
        images = plane_raw[:, pl.ds(a * rows, rows)].T
        wide = images.astype(f32)
        inv = 1.0 / jnp.sqrt(jnp.sum(wide * wide, axis=1, keepdims=True) + eps)
        dots = jnp.dot(images, ring_raw[...], preferred_element_type=f32) * inv * ring_inv
        logits = scale * dots + bias
        plane_id = ((a // CORE * ZL + zl) * CORE + a % CORE) * rows + row
        label = jnp.where(plane_id == ring_id, f32(1.0), f32(-1.0))
        margin = label * logits
        small = jnp.exp(-jnp.abs(margin))
        sigmoid = jnp.where(margin >= 0, small, 1.0) / (1.0 + small)
        pair_grad = -label * sigmoid * f32(1.0 / total)
        inner = pair_grad * dots
        loss += jnp.sum(jnp.log1p(small) - jnp.minimum(margin, 0.0), axis=0, keepdims=True)
        grad_scale += jnp.sum(inner, axis=0, keepdims=True)
        grad_bias += jnp.sum(pair_grad, axis=0, keepdims=True)
        shift = scale * jnp.sum(inner, axis=1, keepdims=True) * inv
        shift = jnp.broadcast_to(shift, (rows, rows)).T[:1]
        inv = jnp.broadcast_to(inv, (rows, rows)).T[:1]
        coef = (scale * pair_grad * ring_inv).astype(bf16)
        draw = lax.dot_general(
            ring_own, coef, (((1,), (1,)), ((), ())), preferred_element_type=f32
        )
        raw = plane_raw[pl.ds(own_at, own), pl.ds(a * rows, rows)].astype(f32)
        draw = ((draw - raw * shift) * inv).astype(bf16)
        for b in range(Y):
            part = draw[b * feats : (b + 1) * feats]
            out[a // CORE * Y + b, pl.ds(0, feats), pl.ds(a % CORE * rows, rows)] = part

    lane = lax.broadcasted_iota(jnp.int32, (TAIL, CORE * rows), 1)
    tail = jnp.zeros((TAIL, CORE * rows), f32)
    for k, value in enumerate((loss * f32(1.0 / total), grad_scale, grad_bias)):
        for n, part in enumerate(in_parts(jnp.sum(value, axis=1, keepdims=True))):
            tail = jnp.where(lane == 3 * k + n, part, tail)
    for s in range(X * Y):
        out[s, pl.ds(feats, TAIL), :] = tail.astype(bf16)


def row_gradients(place, factors, plane, ring, ring_other):
    feats, rows = ring.shape[1:]
    smem, vmem = pl.BlockSpec(memory_space=pltpu.SMEM), pl.BlockSpec(memory_space=pltpu.VMEM)
    emb, block = feats * ZH * Y, rows * X
    return pl.pallas_call(
        pairs_kernel,
        out_shape=jax.ShapeDtypeStruct((X * Y, feats + TAIL, CORE * rows), jnp.bfloat16),
        in_specs=[smem] * 2 + [vmem] * 3,
        out_specs=vmem,
        scratch_shapes=[
            pltpu.VMEM((emb, CORE * block), jnp.bfloat16),
            pltpu.VMEM((emb, block), jnp.bfloat16),
        ],
        compiler_params=pltpu.CompilerParams(vmem_limit_bytes=48 * 1024 * 1024),
    )(place, factors, plane, ring, ring_other)


def shards(image_pooled, text_pooled, image_proj, text_proj, logit_scale, logit_bias):
    bf16, f32 = jnp.bfloat16, jnp.float32
    x, zl, core, zh, y = [lax.axis_index(a) for a in AXES]
    width = image_pooled.shape[1]
    feats = image_proj.shape[0]
    place = jnp.stack([core, x, y, zl, zh]).astype(jnp.int32)
    factors = jnp.stack([logit_scale, logit_bias])
    first = core == 0

    def raw_of(proj, pooled):
        return lax.dot_general(
            proj, pooled, (((1,), (1,)), ((), ())), preferred_element_type=f32
        ).astype(bf16)

    to_ring = [(p * Y + q, (p % 2 * Y + q) * Y + p // 2) for p in range(ZL) for q in range(Y)]
    pooled = jnp.where(first, image_pooled, text_pooled)
    beside = swap(jnp.where(first, text_pooled, image_pooled), "core")
    pooled = jnp.concatenate([jnp.where(first, pooled, beside), jnp.where(first, beside, pooled)])
    image_raw, text_raw = raw_of(image_proj, image_pooled), raw_of(text_proj, text_pooled)
    mine, theirs = jnp.where(first, image_raw, text_raw), jnp.where(first, text_raw, image_raw)
    raw = jnp.concatenate([mine, theirs])
    ring = lax.ppermute(raw, ("zl", "y"), to_ring)
    far = swap(raw, "zh")
    low = zh == 0

    def both_zh(here, there):
        return jnp.concatenate([jnp.where(low, here, there), jnp.where(low, there, here)])

    beside = swap(both_zh(theirs, far[feats:]), "core")
    ring_first, ring_second = ring[feats:], swap(ring[:feats], "core")
    plane = both_zh(mine, far[:feats])
    plane = jnp.concatenate([jnp.where(first, plane, beside), jnp.where(first, beside, plane)])
    plane, ring_first, ring_second, pooled = lax.optimization_barrier(
        (plane, ring_first, ring_second, pooled)
    )
    plane = spread(plane, ("x", "y"), X * Y)
    ring_first = lax.all_gather(ring_first, ("zh", "zl"), axis=0, tiled=False)
    ring_second = lax.all_gather(ring_second, ("zh", "zl"), axis=0, tiled=False)
    plane, ring_first, ring_second = lax.optimization_barrier((plane, ring_first, ring_second))
    parts = row_gradients(place, factors, plane, ring_first, ring_second)
    parts = lax.all_to_all(parts, ("x", "y"), 0, 0, tiled=True)
    parts = jnp.sum(parts.astype(f32), axis=0)
    draw, tail = parts[:feats].astype(bf16), parts[feats : feats + 8, :128]
    tail = jnp.where(first, tail, swap(tail, "core"))

    weight = jnp.dot(draw, pooled, preferred_element_type=f32)

    count = (feats // 8) * (width // 128)
    share = -(-count // (X * ZL))
    tiles = weight.astype(bf16).reshape(feats // 8, 8, width // 128, 128).transpose(0, 2, 1, 3)
    tiles = jnp.pad(tiles.reshape(count, 8, 128), ((0, X * ZL * share - count), (0, 0), (0, 0)))
    tiles = lax.all_to_all(tiles.reshape(X, ZL * share, 8, 128), "x", 0, 0, tiled=True)
    tiles = jnp.sum(tiles.astype(f32), axis=0).reshape(ZL, share, 8, 128)
    tiles = jnp.concatenate([tiles, jnp.broadcast_to(tail, (ZL, 1, 8, 128))], axis=1)
    tiles = jnp.sum(lax.all_to_all(tiles, "zl", 0, 0, tiled=True), axis=0)
    tail = tiles[share]
    sums = tail[0, :9].reshape(3, 3).sum(axis=1)
    tiles = spread(tiles[:share].astype(bf16), "zl", ZL)
    tiles = lax.all_gather(tiles, "x", axis=0, tiled=False)
    other = swap(tiles, "core")

    def whole(tiles):
        tiles = tiles.reshape(X * ZL * share, 8, 128)[:count]
        tiles = tiles.reshape(feats // 8, width // 128, 8, 128).transpose(0, 2, 1, 3)
        return tiles.reshape(feats, width).astype(f32)

    image_grad = whole(jnp.where(first, tiles, other))
    text_grad = whole(jnp.where(first, other, tiles))
    return (sums[0], sums[1], sums[2], image_grad, text_grad)


def solution(mesh):
    fine = Mesh(mesh.devices.reshape(X, ZL, CORE, ZH, Y), AXES)
    dp, tensor = ("x", "zl", "core"), ("zh", "y")
    placed = (P(dp, None), P(dp, None), P(tensor, None), P(tensor, None), P(), P())
    return jax.shard_map(
        shards,
        mesh=fine,
        in_specs=placed,
        out_specs=(P(), P(), P(), P(tensor, None), P(tensor, None)),
        check_vma=False,
    )
```

```python
import jax
import jax.numpy as jnp
from jax import lax
from jax.experimental import pallas as pl
from jax.experimental.pallas import tpu as pltpu
from jax.sharding import Mesh, PartitionSpec as P

eps = 1e-06
X, ZL, CORE, ZH, Y = 4, 8, 2, 2, 4
AXES = ("x", "zl", "core", "zh", "y")
TAIL = 16


def swap(block, axis):
    return lax.ppermute(block, axis, [(0, 1), (1, 0)])


def spread(block, axes, count):
    copies = jnp.broadcast_to(block[None], (count,) + block.shape)
    return lax.all_to_all(copies, axes, 0, 0, tiled=True)


def in_parts(value):
    high = value.astype(jnp.bfloat16).astype(jnp.float32)
    rest = value - high
    mid = rest.astype(jnp.bfloat16).astype(jnp.float32)
    return high, mid, rest - mid


def pairs_kernel(
    place, factors, plane, ring_mine, ring_other, out, plane_raw, ring_raw
):
    bf16, f32 = jnp.bfloat16, jnp.float32
    core, x, y, zl, zh = [place[k] for k in range(5)]
    scale, bias = factors[0], factors[1]
    feats, rows = ring_mine.shape[1:]
    emb, block = ring_raw.shape
    own = emb // ZH
    total = rows * X * ZL * CORE

    for s in range(X * Y):
        for g in range(CORE):
            lanes = pl.ds((s // Y * CORE + g) * rows, rows)
            for h in range(ZH):
                piece = plane[s, pl.ds((g * ZH + h) * feats, feats), :]
                plane_raw[pl.ds((h * Y + s % Y) * feats, feats), lanes] = piece
    for ref, owner in ((ring_mine, core), (ring_other, 1 - core)):
        for s in range(ZH * ZL):
            at = (s // ZL * Y + s % Y) * feats
            lanes = pl.multiple_of((s % ZL // Y * CORE + owner) * rows, rows)
            ring_raw[pl.ds(at, feats), pl.ds(lanes, rows)] = ref[s]

    wide = ring_raw[...].astype(f32)
    ring_inv = 1.0 / jnp.sqrt(jnp.sum(wide * wide, axis=0, keepdims=True) + eps)
    own_at = pl.multiple_of(zh * own, 16)
    ring_own = ring_raw[pl.ds(own_at, own), :]

    pair = CORE * rows
    lane = lax.broadcasted_iota(jnp.int32, (pair, block), 1)
    row = lax.broadcasted_iota(jnp.int32, (pair, block), 0)
    ring_id = ((x * ZL + 2 * y) * CORE + lane // rows) * rows + lane % rows
    loss = grad_scale = grad_bias = jnp.zeros((1, block), f32)
    for a in range(X):
        images = plane_raw[:, pl.ds(a * pair, pair)].T
        wide = images.astype(f32)
        inv = 1.0 / jnp.sqrt(jnp.sum(wide * wide, axis=1, keepdims=True) + eps)
        dots = jnp.dot(images, ring_raw[...], preferred_element_type=f32) * inv * ring_inv
        logits = scale * dots + bias
        plane_id = (a * ZL + zl) * pair + row
        label = jnp.where(plane_id == ring_id, f32(1.0), f32(-1.0))
        margin = label * logits
        small = jnp.exp(-jnp.abs(margin))
        sigmoid = jnp.where(margin >= 0, small, 1.0) / (1.0 + small)
        pair_grad = -label * sigmoid * f32(1.0 / total)
        inner = pair_grad * dots
        loss += jnp.sum(jnp.log1p(small) - jnp.minimum(margin, 0.0), axis=0, keepdims=True)
        grad_scale += jnp.sum(inner, axis=0, keepdims=True)
        grad_bias += jnp.sum(pair_grad, axis=0, keepdims=True)
        shift = scale * jnp.sum(inner, axis=1, keepdims=True) * inv
        shift = jnp.broadcast_to(shift, (pair, rows)).T[:1]
        inv = jnp.broadcast_to(inv, (pair, rows)).T[:1]
        coef = (scale * pair_grad * ring_inv).astype(bf16)
        draw = lax.dot_general(
            ring_own, coef, (((1,), (1,)), ((), ())), preferred_element_type=f32
        )
        raw = plane_raw[pl.ds(own_at, own), pl.ds(a * pair, pair)].astype(f32)
        draw = ((draw - raw * shift) * inv).astype(bf16)
        for b in range(Y):
            part = draw[b * feats : (b + 1) * feats]
            out[a * Y + b, pl.ds(0, feats), :] = part

    lane = lax.broadcasted_iota(jnp.int32, (TAIL, CORE * rows), 1)
    tail = jnp.zeros((TAIL, CORE * rows), f32)
    for k, value in enumerate((loss * f32(1.0 / total), grad_scale, grad_bias)):
        for n, part in enumerate(in_parts(jnp.sum(value, axis=1, keepdims=True))):
            tail = jnp.where(lane == 3 * k + n, part, tail)
    for s in range(X * Y):
        out[s, pl.ds(feats, TAIL), :] = tail.astype(bf16)


def row_gradients(place, factors, plane, ring, ring_other):
    feats, rows = ring.shape[1:]
    smem, vmem = pl.BlockSpec(memory_space=pltpu.SMEM), pl.BlockSpec(memory_space=pltpu.VMEM)
    emb, block = feats * ZH * Y, rows * X
    return pl.pallas_call(
        pairs_kernel,
        out_shape=jax.ShapeDtypeStruct((X * Y, feats + TAIL, CORE * rows), jnp.bfloat16),
        in_specs=[smem] * 2 + [vmem] * 3,
        out_specs=vmem,
        scratch_shapes=[
            pltpu.VMEM((emb, CORE * block), jnp.bfloat16),
            pltpu.VMEM((emb, block), jnp.bfloat16),
        ],
        compiler_params=pltpu.CompilerParams(vmem_limit_bytes=48 * 1024 * 1024),
    )(place, factors, plane, ring, ring_other)


def shards(image_pooled, text_pooled, image_proj, text_proj, logit_scale, logit_bias):
    bf16, f32 = jnp.bfloat16, jnp.float32
    x, zl, core, zh, y = [lax.axis_index(a) for a in AXES]
    width = image_pooled.shape[1]
    feats = image_proj.shape[0]
    place = jnp.stack([core, x, y, zl, zh]).astype(jnp.int32)
    factors = jnp.stack([logit_scale, logit_bias])
    first = core == 0

    def raw_of(proj, pooled):
        return lax.dot_general(
            proj, pooled, (((1,), (1,)), ((), ())), preferred_element_type=f32
        ).astype(bf16)

    to_ring = [(p * Y + q, (p % 2 * Y + q) * Y + p // 2) for p in range(ZL) for q in range(Y)]
    pooled = jnp.where(first, image_pooled, text_pooled)
    beside = swap(jnp.where(first, text_pooled, image_pooled), "core")
    pooled = jnp.concatenate([jnp.where(first, pooled, beside), jnp.where(first, beside, pooled)])
    image_raw, text_raw = raw_of(image_proj, image_pooled), raw_of(text_proj, text_pooled)
    mine, theirs = jnp.where(first, image_raw, text_raw), jnp.where(first, text_raw, image_raw)
    raw = jnp.concatenate([mine, theirs])
    ring = lax.ppermute(raw, ("zl", "y"), to_ring)
    far = swap(raw, "zh")
    low = zh == 0

    def both_zh(here, there):
        return jnp.concatenate([jnp.where(low, here, there), jnp.where(low, there, here)])

    beside = swap(both_zh(theirs, far[feats:]), "core")
    ring_first, ring_second = ring[feats:], swap(ring[:feats], "core")
    plane = both_zh(mine, far[:feats])
    plane = jnp.concatenate([jnp.where(first, plane, beside), jnp.where(first, beside, plane)])
    plane, ring_first, ring_second, pooled = lax.optimization_barrier(
        (plane, ring_first, ring_second, pooled)
    )
    plane = spread(plane, ("x", "y"), X * Y)
    ring_first = lax.all_gather(ring_first, ("zh", "zl"), axis=0, tiled=False)
    ring_second = lax.all_gather(ring_second, ("zh", "zl"), axis=0, tiled=False)
    plane, ring_first, ring_second = lax.optimization_barrier((plane, ring_first, ring_second))
    parts = row_gradients(place, factors, plane, ring_first, ring_second)
    parts = lax.all_to_all(parts, ("x", "y"), 0, 0, tiled=True)
    parts = jnp.sum(parts.astype(f32), axis=0)
    draw, tail = parts[:feats].astype(bf16), parts[feats : feats + 8, :128]
    tail = jnp.where(first, tail, swap(tail, "core"))

    weight = jnp.dot(draw, pooled, preferred_element_type=f32)

    count = (feats // 8) * (width // 128)
    share = -(-count // (X * ZL))
    tiles = weight.astype(bf16).reshape(feats // 8, 8, width // 128, 128).transpose(0, 2, 1, 3)
    tiles = jnp.pad(tiles.reshape(count, 8, 128), ((0, X * ZL * share - count), (0, 0), (0, 0)))
    tiles = lax.all_to_all(tiles.reshape(X, ZL * share, 8, 128), "x", 0, 0, tiled=True)
    tiles = jnp.sum(tiles.astype(f32), axis=0).reshape(ZL, share, 8, 128)
    tiles = jnp.concatenate([tiles, jnp.broadcast_to(tail, (ZL, 1, 8, 128))], axis=1)
    tiles = jnp.sum(lax.all_to_all(tiles, "zl", 0, 0, tiled=True), axis=0)
    tail = tiles[share]
    sums = tail[0, :9].reshape(3, 3).sum(axis=1)
    tiles = spread(tiles[:share].astype(bf16), "zl", ZL)
    tiles = lax.all_gather(tiles, "x", axis=0, tiled=False)
    other = swap(tiles, "core")

    def whole(tiles):
        tiles = tiles.reshape(X * ZL * share, 8, 128)[:count]
        tiles = tiles.reshape(feats // 8, width // 128, 8, 128).transpose(0, 2, 1, 3)
        return tiles.reshape(feats, width).astype(f32)

    image_grad = whole(jnp.where(first, tiles, other))
    text_grad = whole(jnp.where(first, other, tiles))
    return (sums[0], sums[1], sums[2], image_grad, text_grad)


def solution(mesh):
    fine = Mesh(mesh.devices.reshape(X, ZL, CORE, ZH, Y), AXES)
    dp, tensor = ("x", "zl", "core"), ("zh", "y")
    placed = (P(dp, None), P(dp, None), P(tensor, None), P(tensor, None), P(), P())
    return jax.shard_map(
        shards,
        mesh=fine,
        in_specs=placed,
        out_specs=(P(), P(), P(), P(tensor, None), P(tensor, None)),
        check_vma=False,
    )
```

```python
import jax
import jax.numpy as jnp
from jax import lax
from jax.experimental import pallas as pl
from jax.experimental.pallas import tpu as pltpu
from jax.sharding import Mesh, PartitionSpec as P

eps = 1e-06
X, ZL, CORE, ZH, Y = 4, 8, 2, 2, 4
AXES = ("x", "zl", "core", "zh", "y")
TAIL = 16


def swap(block, axis):
    return lax.ppermute(block, axis, [(0, 1), (1, 0)])


def spread(block, axes, count):
    copies = jnp.broadcast_to(block[None], (count,) + block.shape)
    return lax.all_to_all(copies, axes, 0, 0, tiled=True)


def in_parts(value):
    high = value.astype(jnp.bfloat16).astype(jnp.float32)
    rest = value - high
    mid = rest.astype(jnp.bfloat16).astype(jnp.float32)
    return high, mid, rest - mid


def pairs_kernel(
    place, factors, plane, ring_mine, ring_other, out, plane_raw, ring_raw
):
    bf16, f32 = jnp.bfloat16, jnp.float32
    core, x, y, zl, zh = [place[k] for k in range(5)]
    scale, bias = factors[0], factors[1]
    feats, rows = ring_mine.shape[1:]
    emb, block = ring_raw.shape
    own = emb // ZH
    total = rows * X * ZL * CORE

    for s in range(X * Y):
        for g, owner in enumerate((core, 1 - core)):
            lanes = pl.ds(pl.multiple_of((s // Y * CORE + owner) * rows, rows), rows)
            for h, half in enumerate((zh, 1 - zh)):
                at = pl.multiple_of((half * Y + s % Y) * feats, 16)
                piece = plane[s, pl.ds((g * ZH + h) * feats, feats), :]
                plane_raw[pl.ds(at, feats), lanes] = piece
    for ref, owner in ((ring_mine, core), (ring_other, 1 - core)):
        for s in range(ZH * ZL):
            at = (s // ZL * Y + s % Y) * feats
            lanes = pl.multiple_of((s % ZL // Y * CORE + owner) * rows, rows)
            ring_raw[pl.ds(at, feats), pl.ds(lanes, rows)] = ref[s]

    wide = ring_raw[...].astype(f32)
    ring_inv = 1.0 / jnp.sqrt(jnp.sum(wide * wide, axis=0, keepdims=True) + eps)
    own_at = pl.multiple_of(zh * own, 16)
    ring_own = ring_raw[pl.ds(own_at, own), :]

    pair = CORE * rows
    lane = lax.broadcasted_iota(jnp.int32, (pair, block), 1)
    row = lax.broadcasted_iota(jnp.int32, (pair, block), 0)
    ring_id = ((x * ZL + 2 * y) * CORE + lane // rows) * rows + lane % rows
    loss = grad_scale = grad_bias = jnp.zeros((1, block), f32)
    for a in range(X):
        images = plane_raw[:, pl.ds(a * pair, pair)].T
        wide = images.astype(f32)
        inv = 1.0 / jnp.sqrt(jnp.sum(wide * wide, axis=1, keepdims=True) + eps)
        dots = jnp.dot(images, ring_raw[...], preferred_element_type=f32) * inv * ring_inv
        logits = scale * dots + bias
        plane_id = (a * ZL + zl) * pair + row
        label = jnp.where(plane_id == ring_id, f32(1.0), f32(-1.0))
        margin = label * logits
        small = jnp.exp(-jnp.abs(margin))
        sigmoid = jnp.where(margin >= 0, small, 1.0) / (1.0 + small)
        pair_grad = -label * sigmoid * f32(1.0 / total)
        inner = pair_grad * dots
        loss += jnp.sum(jnp.log1p(small) - jnp.minimum(margin, 0.0), axis=0, keepdims=True)
        grad_scale += jnp.sum(inner, axis=0, keepdims=True)
        grad_bias += jnp.sum(pair_grad, axis=0, keepdims=True)
        shift = scale * jnp.sum(inner, axis=1, keepdims=True) * inv
        shift = jnp.broadcast_to(shift, (pair, rows)).T[:1]
        inv = jnp.broadcast_to(inv, (pair, rows)).T[:1]
        coef = (scale * pair_grad * ring_inv).astype(bf16)
        draw = lax.dot_general(
            ring_own, coef, (((1,), (1,)), ((), ())), preferred_element_type=f32
        )
        raw = plane_raw[pl.ds(own_at, own), pl.ds(a * pair, pair)].astype(f32)
        draw = ((draw - raw * shift) * inv).astype(bf16)
        for b in range(Y):
            part = draw[b * feats : (b + 1) * feats]
            out[a * Y + b, pl.ds(0, feats), :] = part

    lane = lax.broadcasted_iota(jnp.int32, (TAIL, CORE * rows), 1)
    tail = jnp.zeros((TAIL, CORE * rows), f32)
    for k, value in enumerate((loss * f32(1.0 / total), grad_scale, grad_bias)):
        for n, part in enumerate(in_parts(jnp.sum(value, axis=1, keepdims=True))):
            tail = jnp.where(lane == 3 * k + n, part, tail)
    for s in range(X * Y):
        out[s, pl.ds(feats, TAIL), :] = tail.astype(bf16)


def row_gradients(place, factors, plane, ring, ring_other):
    feats, rows = ring.shape[1:]
    smem, vmem = pl.BlockSpec(memory_space=pltpu.SMEM), pl.BlockSpec(memory_space=pltpu.VMEM)
    emb, block = feats * ZH * Y, rows * X
    return pl.pallas_call(
        pairs_kernel,
        out_shape=jax.ShapeDtypeStruct((X * Y, feats + TAIL, CORE * rows), jnp.bfloat16),
        in_specs=[smem] * 2 + [vmem] * 3,
        out_specs=vmem,
        scratch_shapes=[
            pltpu.VMEM((emb, CORE * block), jnp.bfloat16),
            pltpu.VMEM((emb, block), jnp.bfloat16),
        ],
        compiler_params=pltpu.CompilerParams(vmem_limit_bytes=48 * 1024 * 1024),
    )(place, factors, plane, ring, ring_other)


def shards(image_pooled, text_pooled, image_proj, text_proj, logit_scale, logit_bias):
    bf16, f32 = jnp.bfloat16, jnp.float32
    x, zl, core, zh, y = [lax.axis_index(a) for a in AXES]
    width = image_pooled.shape[1]
    feats = image_proj.shape[0]
    place = jnp.stack([core, x, y, zl, zh]).astype(jnp.int32)
    factors = jnp.stack([logit_scale, logit_bias])
    first = core == 0

    def raw_of(proj, pooled):
        return lax.dot_general(
            proj, pooled, (((1,), (1,)), ((), ())), preferred_element_type=f32
        ).astype(bf16)

    to_ring = [(p * Y + q, (p % 2 * Y + q) * Y + p // 2) for p in range(ZL) for q in range(Y)]
    pooled = jnp.where(first, image_pooled, text_pooled)
    beside = swap(jnp.where(first, text_pooled, image_pooled), "core")
    pooled = jnp.concatenate([jnp.where(first, pooled, beside), jnp.where(first, beside, pooled)])
    image_raw, text_raw = raw_of(image_proj, image_pooled), raw_of(text_proj, text_pooled)
    mine, theirs = jnp.where(first, image_raw, text_raw), jnp.where(first, text_raw, image_raw)
    raw = jnp.concatenate([mine, theirs])
    ring = lax.ppermute(raw, ("zl", "y"), to_ring)
    far = swap(raw, "zh")
    beside = swap(jnp.concatenate([theirs, far[feats:]]), "core")
    ring_first, ring_second = ring[feats:], swap(ring[:feats], "core")
    plane = jnp.concatenate([mine, far[:feats], beside])
    plane, ring_first, ring_second, pooled = lax.optimization_barrier(
        (plane, ring_first, ring_second, pooled)
    )
    plane = spread(plane, ("x", "y"), X * Y)
    ring_first = lax.all_gather(ring_first, ("zh", "zl"), axis=0, tiled=False)
    ring_second = lax.all_gather(ring_second, ("zh", "zl"), axis=0, tiled=False)
    plane, ring_first, ring_second = lax.optimization_barrier((plane, ring_first, ring_second))
    parts = row_gradients(place, factors, plane, ring_first, ring_second)
    parts = lax.all_to_all(parts, ("x", "y"), 0, 0, tiled=True)
    parts = jnp.sum(parts.astype(f32), axis=0)
    draw, tail = parts[:feats].astype(bf16), parts[feats : feats + 8, :128]
    tail = jnp.where(first, tail, swap(tail, "core"))

    weight = jnp.dot(draw, pooled, preferred_element_type=f32)

    count = (feats // 8) * (width // 128)
    share = -(-count // (X * ZL))
    tiles = weight.astype(bf16).reshape(feats // 8, 8, width // 128, 128).transpose(0, 2, 1, 3)
    tiles = jnp.pad(tiles.reshape(count, 8, 128), ((0, X * ZL * share - count), (0, 0), (0, 0)))
    tiles = lax.all_to_all(tiles.reshape(X, ZL * share, 8, 128), "x", 0, 0, tiled=True)
    tiles = jnp.sum(tiles.astype(f32), axis=0).reshape(ZL, share, 8, 128)
    tiles = jnp.concatenate([tiles, jnp.broadcast_to(tail, (ZL, 1, 8, 128))], axis=1)
    tiles = jnp.sum(lax.all_to_all(tiles, "zl", 0, 0, tiled=True), axis=0)
    tail = tiles[share]
    sums = tail[0, :9].reshape(3, 3).sum(axis=1)
    tiles = spread(tiles[:share].astype(bf16), "zl", ZL)
    tiles = lax.all_gather(tiles, "x", axis=0, tiled=False)
    other = swap(tiles, "core")

    def whole(tiles):
        tiles = tiles.reshape(X * ZL * share, 8, 128)[:count]
        tiles = tiles.reshape(feats // 8, width // 128, 8, 128).transpose(0, 2, 1, 3)
        return tiles.reshape(feats, width).astype(f32)

    image_grad = whole(jnp.where(first, tiles, other))
    text_grad = whole(jnp.where(first, other, tiles))
    return (sums[0], sums[1], sums[2], image_grad, text_grad)


def solution(mesh):
    fine = Mesh(mesh.devices.reshape(X, ZL, CORE, ZH, Y), AXES)
    dp, tensor = ("x", "zl", "core"), ("zh", "y")
    placed = (P(dp, None), P(dp, None), P(tensor, None), P(tensor, None), P(), P())
    return jax.shard_map(
        shards,
        mesh=fine,
        in_specs=placed,
        out_specs=(P(), P(), P(), P(tensor, None), P(tensor, None)),
        check_vma=False,
    )
```
